32 devices in a mesh: front: 4 (over y, x), blk: 8 (over z, core).
Axes of the slice: x: 2, y: 2, z: 4, core: 2. Of those that a mesh axis runs over, the one named last changes fastest.
Arguments:
- front_matrix: float32 [4, 13312, 13312], P('front', 'blk')
- random_probe: float32 [4, 13312, 256], P('front', 'blk'), may hold values from -6 to 6
- child_samples: float32 [4, 3072, 256], P('front', 'blk'), may hold values from -6 to 6
- child_dest: int32 [4, 3072], P('front', 'blk'), may hold values from 0 to 13311, as said below
- skeleton: int32 [4, 8, 128], P('front', 'blk'), may hold values from 0 to 1663, as said below
- leaf_ranks: int32 [4, 8], P('front', 'blk'), may hold values from 64 to 128, as said below
- pair_skeleton: int32 [4, 4, 128], P('front'), may hold values from 0 to 255, as said below
Outputs:
- interp_leaf: float32 [4, 13312, 128], P('front', 'blk')
- interp_pair: float32 [4, 1024, 128], P('front', 'blk')
The draws below stay inside these ranges and needn't reach their ends.
Inputs may be any that keep to these rules, and one draw needn't show every extreme that they name: `child_dest`: among the rows of one device, at most 96 name rows of one leaf node; in every group one leaf node of the next group receives exactly 96 rows from every device of the group. `skeleton`: the 128 entries of one leaf are distinct. `leaf_ranks`: 128 is reached in every front. `pair_skeleton`: the 128 entries of one node are distinct and name live slots only: k of leaf 2q with k below its rank, or 128 + k of leaf 2q+1 with k below its rank.
All inputs are finite; a program needn't handle non-finite values.
Results may differ from the reference program's by a relative error of at most 0.0003.
Values sent between devices are 32-bit elements; how exact they have to be, the bound alone decides.
A program may use at most 192 MiB of HBM per device.

```python
import math
import jax
import jax.numpy as jnp
from jax import lax

NF = 13312
SMP = 256
RMAX = 128
RMIN = 64
R2 = 128
CR_DEV = 384
P_DEV = 1664
CHROWS = 3072
CAP = 96
N_FRONT = 4
N_BLK = 8


def draw_front_matrix(key, part):
    front_keys = jax.random.split(key, N_FRONT)

    def one_front(front_key):
        noise_key, diag_key = jax.random.split(front_key, 2)
        base_noise = jax.random.normal(noise_key, (NF, NF), jnp.float32)
        coupling = (base_noise + base_noise.T) * (2.0 * NF) ** (-0.5)
        diagonal = jnp.exp(jax.random.uniform(diag_key, (NF,), jnp.float32, 0.0, math.log(4.0)))
        positions = jnp.arange(NF)
        return coupling.at[positions, positions].add(diagonal)
    return lax.map(one_front, front_keys)


def draw_child_dest(key, part):

    def one_group(group_key):
        heavy_block = jax.random.randint(jax.random.fold_in(group_key, 0), (), 0, N_BLK)
        block_keys = jax.random.split(jax.random.fold_in(group_key, 1), N_BLK)

        def one_block(block_key):
            score_key, order_key, spot_key = jax.random.split(block_key, 3)
            slot_ids = jnp.arange(N_BLK * CAP, dtype=jnp.int32)
            scores = jax.random.randint(score_key, (N_BLK * CAP,), 1, 2 ** 30)
            scores = jnp.where(slot_ids // CAP == heavy_block, 0, scores)
            taken_slots = jnp.argsort(scores, stable=True)[:CR_DEV].astype(jnp.int32)
            device = jax.random.permutation(order_key, taken_slots // CAP)
            within = jax.random.randint(spot_key, (CR_DEV,), 0, P_DEV)
            return (device * P_DEV + within).astype(jnp.int32)
        return lax.map(one_block, block_keys).reshape(N_BLK * CR_DEV)
    return lax.map(one_group, jax.random.split(key, N_FRONT))


def draw_skeleton(key, part):
    leaf_keys = jax.random.split(jax.random.fold_in(key, 5), N_FRONT * N_BLK)
    pick_rows = jax.vmap(lambda leaf_key: jax.random.permutation(leaf_key, P_DEV)[:RMAX])(leaf_keys)
    return pick_rows.reshape(N_FRONT, N_BLK, RMAX).astype(jnp.int32)


def rank_table(key):
    table_key = jax.random.fold_in(key, 11)
    drawn_ranks = jax.random.randint(jax.random.fold_in(table_key, 1), (N_FRONT, N_BLK), RMIN, RMAX + 1)
    fullest = jax.random.randint(jax.random.fold_in(table_key, 2), (N_FRONT, 1), 0, N_BLK)
    return jnp.where(jnp.arange(N_BLK)[None, :] == fullest, RMAX, drawn_ranks).astype(jnp.int32)


def draw_leaf_ranks(key, part):
    return rank_table(key)


def draw_pair_skeleton(key, part):
    rank_grid = rank_table(key)
    paired = rank_grid.reshape(N_FRONT, N_BLK // 2, 2)
    slot_ids = jnp.arange(2 * RMAX, dtype=jnp.int32)
    live_slots = jnp.where(slot_ids < RMAX, slot_ids < paired[..., 0:1], slot_ids - RMAX < paired[..., 1:2])
    scores = jax.random.randint(jax.random.fold_in(key, 23), (N_FRONT, N_BLK // 2, 2 * RMAX), 1, 2 ** 30)
    scores = jnp.where(live_slots, scores, 2 ** 30)
    return jnp.argsort(scores, axis=-1, stable=True)[..., :R2].astype(jnp.int32)


def levels(key, dims, pieces, smallest, top_value):
    factor_of, own = 1.0, jax.random.fold_in(key, 6)
    for position, parts in pieces:
        steps = jnp.exp(jax.random.uniform(jax.random.fold_in(own, position), (parts,), jnp.float32, smallest / len(pieces), top_value / len(pieces)))
        factor_of = factor_of * jnp.repeat(steps, dims[position] // parts).reshape([-1 if axis == position else 1 for axis in range(len(dims))])
    return factor_of


def scatter_about(key, shape, width, most, pieces=(), held_as=jnp.bfloat16):
    drawn = jax.random.normal(key, shape, jnp.float32) * width
    if len(pieces) > 0:
        drawn = levels(key, shape, pieces, -0.22, 0.18) * drawn
    return jnp.clip(drawn, min=-most, max=most).astype(held_as)


def setup_inputs(seed: int = 0) -> dict:
    seeds = jax.random.split(jax.random.key(seed), 8)
    front_matrix = draw_front_matrix(jax.random.fold_in(seeds[7], 71), 0)
    random_probe = scatter_about(seeds[1], (N_FRONT, NF, SMP), 1.0, 6.0, ((0, 4), (1, 8)), jnp.float32)
    child_samples = scatter_about(seeds[2], (N_FRONT, CHROWS, SMP), 1.0, 6.0, ((0, 4), (1, 8)), jnp.float32)
    child_dest = draw_child_dest(jax.random.fold_in(seeds[7], 71), 0)
    skeleton = draw_skeleton(jax.random.fold_in(seeds[7], 71), 0)
    leaf_ranks = draw_leaf_ranks(jax.random.fold_in(seeds[7], 71), 0)
    pair_skeleton = draw_pair_skeleton(jax.random.fold_in(seeds[7], 71), 0)
    return dict(front_matrix=front_matrix, random_probe=random_probe, child_samples=child_samples, child_dest=child_dest, skeleton=skeleton, leaf_ranks=leaf_ranks, pair_skeleton=pair_skeleton)


HIGHEST = lax.Precision.HIGHEST
ridge_share = 0.1

def exact_dot(left, right):
    return jnp.dot(left.astype(jnp.float32), right.astype(jnp.float32), precision=HIGHEST, preferred_element_type=jnp.float32)

def interpolate(targets, leaf_basis, live_mask, live_count):
    gram_matrix = exact_dot(leaf_basis, leaf_basis.T)
    ridge_size = ridge_share * jnp.sum(jnp.diagonal(gram_matrix)) / live_count
    gram_matrix = gram_matrix + jnp.diag(jnp.where(live_mask, ridge_size, 1.0))
    factor = jnp.linalg.cholesky(gram_matrix)
    cross_terms = exact_dot(targets, leaf_basis.T)
    return jax.scipy.linalg.cho_solve((factor, True), cross_terms.T).T

def leaf_terms(matrix, probe_all, sample, leaf_index, chosen, leaf_rank):
    height = NF // N_BLK
    start_row = leaf_index * height
    row_block = lax.dynamic_slice_in_dim(matrix, start_row, height, 0)
    diagonal_block = lax.dynamic_slice_in_dim(row_block, start_row, height, 1)
    own_probe = lax.dynamic_slice_in_dim(probe_all, start_row, height, 0)
    local_sample = lax.dynamic_slice_in_dim(sample, start_row, height, 0)
    off_sample = local_sample - exact_dot(diagonal_block, own_probe)
    live_mask = jnp.arange(RMAX) < leaf_rank
    leaf_basis = off_sample[chosen] * live_mask[:, None]
    leaf_interp = interpolate(off_sample, leaf_basis, live_mask, leaf_rank.astype(jnp.float32))
    pair_start = leaf_index // 2 * (2 * height)
    pair_columns = lax.dynamic_slice_in_dim(row_block, pair_start, 2 * height, 1)[chosen]
    pair_probe = lax.dynamic_slice_in_dim(probe_all, pair_start, 2 * height, 0)
    upward = (local_sample[chosen] - exact_dot(pair_columns, pair_probe)) * live_mask[:, None]
    return (leaf_interp, upward)

def reference(front_matrix, random_probe, child_samples, child_dest, skeleton, leaf_ranks, pair_skeleton):
    leaf_parts = []
    pair_parts = []
    for front_index in range(N_FRONT):
        source = (front_index - 1) % N_FRONT
        matrix = front_matrix[front_index]
        probe_all = random_probe[front_index]
        sample = exact_dot(matrix, probe_all) + jax.ops.segment_sum(child_samples[source], child_dest[source], num_segments=NF)

        def one_leaf(inputs):
            leaf_index, chosen, leaf_rank = inputs
            return leaf_terms(matrix, probe_all, sample, leaf_index, chosen, leaf_rank)
        leaf_interp, upward = lax.map(one_leaf, (jnp.arange(N_BLK, dtype=jnp.int32), skeleton[front_index], leaf_ranks[front_index]))
        stacked = upward.reshape(N_BLK // 2, 2 * RMAX, SMP)

        def one_pair(inputs):
            targets, pick_rows = inputs
            return interpolate(targets, targets[pick_rows], jnp.ones((R2,), jnp.bool_), float(R2))
        pair_interp = lax.map(one_pair, (stacked, pair_skeleton[front_index]))
        leaf_parts.append(leaf_interp.reshape(NF, RMAX))
        pair_parts.append(pair_interp.reshape(N_BLK * RMAX, R2))
    return (jnp.stack(leaf_parts), jnp.stack(pair_parts))
```

```python
import functools

import jax
import jax.numpy as jnp
from jax import lax
from jax.experimental import pallas as pl
from jax.experimental.pallas import tpu as pltpu
from jax.sharding import PartitionSpec as P

HIGHEST = lax.Precision.HIGHEST
ridge_share = 0.1


def from_behind(value, axis, steps):
    count = lax.axis_size(axis)
    pairs = [(source, (source + steps) % count) for source in range(count)]
    return lax.ppermute(value, axis, pairs)


def from_partner(value, axis, stride):
    mask = 2**stride
    pairs = [(source, source ^ mask) for source in range(lax.axis_size(axis))]
    return lax.ppermute(value, axis, pairs)


def exact_dot(left, right):
    return jnp.dot(left, right, precision=HIGHEST, preferred_element_type=jnp.float32)


def divisor(total, unit, most):
    return max(d for d in range(unit, most + 1, unit) if total % d == 0)


def halves(value):
    high = value.astype(jnp.bfloat16)
    return high, (value - high.astype(jnp.float32)).astype(jnp.bfloat16)


def transposed_kernel(height, sub, me_ref, probe_ref, matrix_ref, out_ref, cat_ref):
    step = pl.program_id(0)
    half = probe_ref.shape[0]
    tile = matrix_ref.shape[1]

    @pl.when(step == 0)
    def _():
        high, low = halves(probe_ref[...])
        cat_ref[pl.ds(0, half), :] = high
        cat_ref[pl.ds(half, half), :] = low

    first = me_ref[0] * height

    def column(index, carry):
        start = pl.multiple_of(index * sub, sub)
        high, low = halves(matrix_ref[:, pl.ds(start, sub)])
        cat = cat_ref[...]
        part = jnp.dot(cat, high, preferred_element_type=jnp.float32)
        part = part + jnp.dot(cat, low, preferred_element_type=jnp.float32)
        rows = (part[:half] + part[half:]).T
        place = step * tile + start + lax.broadcasted_iota(jnp.int32, rows.shape, 0)
        own = (place >= first) & (place < first + height)
        out_ref[pl.ds(start, sub), :] = jnp.where(own, 0.0, rows)
        return carry

    lax.fori_loop(0, tile // sub, column, 0)


def transposed_product(matrix, probe_t, me):
    height, width = matrix.shape
    half = probe_t.shape[0]
    tile = divisor(width, 256, 1024)
    sub = 256
    return pl.pallas_call(
        functools.partial(transposed_kernel, height, sub),
        grid=(width // tile,),
        in_specs=[
            pl.BlockSpec(memory_space=pltpu.SMEM),
            pl.BlockSpec((half, height), lambda i: (0, 0)),
            pl.BlockSpec((height, tile), lambda i: (0, i)),
        ],
        out_specs=pl.BlockSpec((tile, half), lambda i: (i, 0)),
        out_shape=jax.ShapeDtypeStruct((width, half), jnp.float32),
        scratch_shapes=[pltpu.VMEM((2 * half, height), jnp.bfloat16)],
        compiler_params=pltpu.CompilerParams(vmem_limit_bytes=48 * 2**20),
        cost_estimate=pl.CostEstimate(
            flops=8 * height * width * half,
            bytes_accessed=4 * height * width,
            transcendentals=0,
        ),
        name="transposed_product",
    )(me, probe_t, matrix)


def forward_kernel(height, chunk, me_ref, probe_ref, matrix_ref, out_ref, total_ref, cat_ref):
    step = pl.program_id(0)
    tile, half = probe_ref.shape
    first = me_ref[0] * height
    place = step * tile + lax.broadcasted_iota(jnp.int32, (tile, half), 0)
    own = (place >= first) & (place < first + height)
    probe_high, probe_low = halves(jnp.where(own, 0.0, probe_ref[...]))
    cat_ref[:, pl.ds(0, half)] = probe_high
    cat_ref[:, pl.ds(half, half)] = probe_low

    @pl.when(step == 0)
    def _():
        total_ref[...] = jnp.zeros_like(total_ref)

    def rows(index, carry):
        span = pl.ds(pl.multiple_of(index * chunk, chunk), chunk)
        high, low = halves(matrix_ref[span, :])
        cat = cat_ref[...]
        part = jnp.dot(high, cat, preferred_element_type=jnp.float32)
        part = part + jnp.dot(low, cat, preferred_element_type=jnp.float32)
        total_ref[span, :] += part
        return carry

    lax.fori_loop(0, height // chunk, rows, 0)

    @pl.when(step == pl.num_programs(0) - 1)
    def _():
        out_ref[...] = total_ref[:, pl.ds(0, half)] + total_ref[:, pl.ds(half, half)]


def forward_product(matrix, probe, me):
    height, width = matrix.shape
    half = probe.shape[1]
    tile = divisor(width, 256, 1024)
    chunk = divisor(height, 16, 512)
    return pl.pallas_call(
        functools.partial(forward_kernel, height, chunk),
        grid=(width // tile,),
        in_specs=[
            pl.BlockSpec(memory_space=pltpu.SMEM),
            pl.BlockSpec((tile, half), lambda i: (i, 0)),
            pl.BlockSpec((height, tile), lambda i: (0, i)),
        ],
        out_specs=pl.BlockSpec((height, half), lambda i: (0, 0)),
        out_shape=jax.ShapeDtypeStruct((height, half), jnp.float32),
        scratch_shapes=[
            pltpu.VMEM((height, 2 * half), jnp.float32),
            pltpu.VMEM((tile, 2 * half), jnp.bfloat16),
        ],
        compiler_params=pltpu.CompilerParams(vmem_limit_bytes=48 * 2**20),
        cost_estimate=pl.CostEstimate(
            flops=8 * height * width * half,
            bytes_accessed=4 * height * width,
            transcendentals=0,
        ),
        name="forward_product",
    )(me, probe, matrix)


def last_dims(left, right):
    return lax.dot_general(
        left,
        right,
        (((1,), (1,)), ((), ())),
        precision=HIGHEST,
        preferred_element_type=jnp.float32,
    )


def ridged(basis, live, count, row_ids, lane_ids):
    gram = last_dims(basis, basis)
    diagonal = row_ids == lane_ids
    trace = jnp.sum(jnp.where(diagonal, gram, 0.0))
    ridge = ridge_share * trace / count
    return gram + jnp.where(diagonal, jnp.where(row_ids < live, ridge, 1.0), 0.0)


def eliminate(state, k, row_ids, lane_ids):
    at_row = row_ids == k
    at_lane = lane_ids == k
    row = jnp.sum(jnp.where(at_row, state, 0.0), axis=0, keepdims=True)
    column = jnp.sum(jnp.where(at_lane, state, 0.0), axis=1, keepdims=True)
    pivot = jnp.sum(jnp.where(at_lane[:1], row, 0.0), axis=1, keepdims=True)
    inverse = 1.0 / pivot
    row = jnp.where(at_lane[:1], inverse, row * inverse)
    rest = jnp.where(at_lane, 0.0, state) - column * row
    return jnp.where(at_row, row, rest)


def interpolate_kernel(
    rank_ref, off_ref, basis_ref, upward_ref, pair_ref, leaf_out_ref, pair_out_ref
):
    slots = basis_ref.shape[0]
    width = pair_ref.shape[0]
    rank = rank_ref[0]
    row_ids = lax.broadcasted_iota(jnp.int32, (slots, slots), 0)
    lane_ids = lax.broadcasted_iota(jnp.int32, (slots, slots), 1)
    basis = basis_ref[...]
    pair = pair_ref[...]
    leaf_state = ridged(basis, rank, rank.astype(jnp.float32), row_ids, lane_ids)
    pair_state = ridged(pair, width, float(width), row_ids, lane_ids)

    def step(k, states):
        return tuple(eliminate(state, k, row_ids, lane_ids) for state in states)

    leaf_state, pair_state = lax.fori_loop(0, slots, step, (leaf_state, pair_state))
    leaf_weights = jnp.dot(
        leaf_state, basis, precision=HIGHEST, preferred_element_type=jnp.float32
    )
    pair_weights = jnp.dot(pair_state, pair, precision=HIGHEST, preferred_element_type=jnp.float32)
    pair_out_ref[...] = last_dims(upward_ref[...], pair_weights)
    leaf_out_ref[...] = last_dims(off_ref[...], leaf_weights)


def interpolate_both(rank, off, basis, upward, pair):
    vmem = pl.BlockSpec(memory_space=pltpu.VMEM)
    return pl.pallas_call(
        interpolate_kernel,
        in_specs=[pl.BlockSpec(memory_space=pltpu.SMEM)] + [vmem] * 4,
        out_specs=[vmem] * 2,
        out_shape=[
            jax.ShapeDtypeStruct((off.shape[0], basis.shape[0]), jnp.float32),
            jax.ShapeDtypeStruct((upward.shape[0], pair.shape[0]), jnp.float32),
        ],
        compiler_params=pltpu.CompilerParams(vmem_limit_bytes=32 * 2**20),
        name="interpolate_both",
    )(rank, off, basis, upward, pair)


def body(
    front_matrix, random_probe, child_samples, child_dest, skeleton, leaf_ranks, pair_skeleton
):
    matrix = front_matrix[0]
    own_probe = random_probe[0]
    height = matrix.shape[0]
    samples = own_probe.shape[1]
    half = samples // 2
    leaf_index = lax.axis_index("blk")
    me = leaf_index.astype(jnp.int32)[None]
    pair_index = leaf_index // 2
    lower_half = leaf_index % 2 == 0

    gathered = lax.all_gather(own_probe[:, :half], "blk", axis=0, tiled=True)
    partial = transposed_product(matrix, own_probe[:, half:].T, me)
    upper_columns = lax.psum_scatter(partial, "blk", scatter_dimension=0, tiled=True)
    sibling_probe = from_partner(own_probe, "blk", 0)

    blocks = lax.axis_size("blk")
    incoming = child_samples[0]
    destinations = child_dest[0]
    count_rows = incoming.shape[0]
    capacity = max(2, (2 * count_rows + blocks - 1) // blocks)
    owner_block = destinations // height
    within = (destinations % height).astype(jnp.float32)
    order = jnp.arange(count_rows, dtype=jnp.int32)
    earlier = (owner_block[:, None] == owner_block[None, :]) & (order[None, :] < order[:, None])
    ranking = jnp.sum(earlier.astype(jnp.int32), axis=1)
    places = owner_block * capacity + ranking
    slots_total = blocks * capacity
    sending = jnp.zeros((slots_total, samples), jnp.float32).at[places].set(incoming)
    labels = jnp.full((slots_total,), float(height), jnp.float32).at[places].set(within)
    spread_rows, spread_labels = (
        lax.all_to_all(sending, "blk", split_axis=0, concat_axis=0, tiled=True),
        lax.all_to_all(labels, "blk", split_axis=0, concat_axis=0, tiled=True),
    )
    arrived, arrived_labels = from_behind((spread_rows, spread_labels), "front", 1)
    child_part = jax.ops.segment_sum(
        arrived, arrived_labels.astype(jnp.int32), num_segments=height + 1
    )[:height]

    chosen = skeleton[0, 0]
    leaf_rank = leaf_ranks[0, 0]
    live_mask = (jnp.arange(chosen.shape[0]) < leaf_rank)[:, None]
    sibling_start = (leaf_index ^ 1) * height
    sibling_columns = lax.dynamic_slice_in_dim(matrix[chosen], sibling_start, height, 1)
    sibling_term = exact_dot(sibling_columns, sibling_probe)

    lower_columns = forward_product(matrix, gathered, me)
    off_sample = jnp.concatenate([lower_columns, upper_columns], axis=1) + child_part
    picked = off_sample[chosen]
    leaf_basis = jnp.where(live_mask, picked, 0.0)
    upward = jnp.where(live_mask, picked - sibling_term, 0.0)
    sibling = from_partner(upward, "blk", 0)
    stacked = jnp.where(
        lower_half, jnp.concatenate([upward, sibling]), jnp.concatenate([sibling, upward])
    )
    pick_rows = lax.dynamic_index_in_dim(pair_skeleton[0], pair_index, 0, keepdims=False)
    pair_basis = stacked[pick_rows]
    leaf_interp, pair_interp = interpolate_both(
        leaf_rank[None], off_sample, leaf_basis, upward, pair_basis
    )
    return (leaf_interp[None], pair_interp[None])


def solution(mesh):
    placed = (
        P("front", "blk", None),
        P("front", "blk", None),
        P("front", "blk", None),
        P("front", "blk"),
        P("front", "blk", None),
        P("front", "blk"),
        P("front", None, None),
    )
    return jax.shard_map(
        body,
        mesh=mesh,
        in_specs=placed,
        out_specs=(P("front", "blk", None), P("front", "blk", None)),
        check_vma=False,
    )
```

```python
import functools

import jax
import jax.numpy as jnp
from jax import lax
from jax.experimental import pallas as pl
from jax.experimental.pallas import tpu as pltpu
from jax.sharding import PartitionSpec as P

HIGHEST = lax.Precision.HIGHEST
ridge_share = 0.1


def from_behind(value, axis, steps):
    count = lax.axis_size(axis)
    pairs = [(source, (source + steps) % count) for source in range(count)]
    return lax.ppermute(value, axis, pairs)


def from_partner(value, axis, stride):
    mask = 2**stride
    pairs = [(source, source ^ mask) for source in range(lax.axis_size(axis))]
    return lax.ppermute(value, axis, pairs)


def exact_dot(left, right):
    return jnp.dot(left, right, precision=HIGHEST, preferred_element_type=jnp.float32)


def divisor(total, unit, most):
    return max(d for d in range(unit, most + 1, unit) if total % d == 0)


def halves(value):
    high = value.astype(jnp.bfloat16)
    return high, (value - high.astype(jnp.float32)).astype(jnp.bfloat16)


def transposed_kernel(height, sub, me_ref, probe_ref, matrix_ref, out_ref, cat_ref):
    step = pl.program_id(0)
    half = probe_ref.shape[0]
    tile = matrix_ref.shape[1]

    @pl.when(step == 0)
    def _():
        high, low = halves(probe_ref[...])
        cat_ref[pl.ds(0, half), :] = high
        cat_ref[pl.ds(half, half), :] = low

    first = me_ref[0] * height

    def column(index, carry):
        start = pl.multiple_of(index * sub, sub)
        high, low = halves(matrix_ref[:, pl.ds(start, sub)])
        cat = cat_ref[...]
        part = jnp.dot(cat, high, preferred_element_type=jnp.float32)
        part = part + jnp.dot(cat, low, preferred_element_type=jnp.float32)
        rows = (part[:half] + part[half:]).T
        place = step * tile + start + lax.broadcasted_iota(jnp.int32, rows.shape, 0)
        own = (place >= first) & (place < first + height)
        out_ref[pl.ds(start, sub), :] = jnp.where(own, 0.0, rows)
        return carry

    lax.fori_loop(0, tile // sub, column, 0)


def transposed_product(matrix, probe_t, me):
    height, width = matrix.shape
    half = probe_t.shape[0]
    tile = divisor(width, 256, 1024)
    sub = 256
    return pl.pallas_call(
        functools.partial(transposed_kernel, height, sub),
        grid=(width // tile,),
        in_specs=[
            pl.BlockSpec(memory_space=pltpu.SMEM),
            pl.BlockSpec((half, height), lambda i: (0, 0)),
            pl.BlockSpec((height, tile), lambda i: (0, i)),
        ],
        out_specs=pl.BlockSpec((tile, half), lambda i: (i, 0)),
        out_shape=jax.ShapeDtypeStruct((width, half), jnp.float32),
        scratch_shapes=[pltpu.VMEM((2 * half, height), jnp.bfloat16)],
        compiler_params=pltpu.CompilerParams(vmem_limit_bytes=48 * 2**20),
        cost_estimate=pl.CostEstimate(
            flops=8 * height * width * half,
            bytes_accessed=4 * height * width,
            transcendentals=0,
        ),
        name="transposed_product",
    )(me, probe_t, matrix)


def forward_kernel(height, chunk, me_ref, probe_ref, matrix_ref, out_ref, total_ref, cat_ref):
    step = pl.program_id(0)
    tile, half = probe_ref.shape
    first = me_ref[0] * height
    place = step * tile + lax.broadcasted_iota(jnp.int32, (tile, half), 0)
    own = (place >= first) & (place < first + height)
    probe_high, probe_low = halves(jnp.where(own, 0.0, probe_ref[...]))
    cat_ref[:, pl.ds(0, half)] = probe_high
    cat_ref[:, pl.ds(half, half)] = probe_low

    @pl.when(step == 0)
    def _():
        total_ref[...] = jnp.zeros_like(total_ref)

    def rows(index, carry):
        span = pl.ds(pl.multiple_of(index * chunk, chunk), chunk)
        high, low = halves(matrix_ref[span, :])
        cat = cat_ref[...]
        part = jnp.dot(high, cat, preferred_element_type=jnp.float32)
        part = part + jnp.dot(low, cat, preferred_element_type=jnp.float32)
        total_ref[span, :] += part
        return carry

    lax.fori_loop(0, height // chunk, rows, 0)

    @pl.when(step == pl.num_programs(0) - 1)
    def _():
        out_ref[...] = total_ref[:, pl.ds(0, half)] + total_ref[:, pl.ds(half, half)]


def forward_product(matrix, probe, me):
    height, width = matrix.shape
    half = probe.shape[1]
    tile = divisor(width, 256, 1024)
    chunk = divisor(height, 16, 512)
    return pl.pallas_call(
        functools.partial(forward_kernel, height, chunk),
        grid=(width // tile,),
        in_specs=[
            pl.BlockSpec(memory_space=pltpu.SMEM),
            pl.BlockSpec((tile, half), lambda i: (i, 0)),
            pl.BlockSpec((height, tile), lambda i: (0, i)),
        ],
        out_specs=pl.BlockSpec((height, half), lambda i: (0, 0)),
        out_shape=jax.ShapeDtypeStruct((height, half), jnp.float32),
        scratch_shapes=[
            pltpu.VMEM((height, 2 * half), jnp.float32),
            pltpu.VMEM((tile, 2 * half), jnp.bfloat16),
        ],
        compiler_params=pltpu.CompilerParams(vmem_limit_bytes=48 * 2**20),
        cost_estimate=pl.CostEstimate(
            flops=8 * height * width * half,
            bytes_accessed=4 * height * width,
            transcendentals=0,
        ),
        name="forward_product",
    )(me, probe, matrix)


def last_dims(left, right):
    return lax.dot_general(
        left,
        right,
        (((1,), (1,)), ((), ())),
        precision=HIGHEST,
        preferred_element_type=jnp.float32,
    )


def ridged(basis, live, count, row_ids, lane_ids):
    gram = last_dims(basis, basis)
    diagonal = row_ids == lane_ids
    trace = jnp.sum(jnp.where(diagonal, gram, 0.0))
    ridge = ridge_share * trace / count
    return gram + jnp.where(diagonal, jnp.where(row_ids < live, ridge, 1.0), 0.0)


def eliminate(state, k, row_ids, lane_ids):
    at_row = row_ids == k
    at_lane = lane_ids == k
    row = jnp.sum(jnp.where(at_row, state, 0.0), axis=0, keepdims=True)
    column = jnp.sum(jnp.where(at_lane, state, 0.0), axis=1, keepdims=True)
    pivot = jnp.sum(jnp.where(at_lane[:1], row, 0.0), axis=1, keepdims=True)
    inverse = 1.0 / pivot
    row = jnp.where(at_lane[:1], inverse, row * inverse)
    rest = jnp.where(at_lane, 0.0, state) - column * row
    return jnp.where(at_row, row, rest)


def interpolate_kernel(
    rank_ref, off_ref, basis_ref, upward_ref, pair_ref, leaf_out_ref, pair_out_ref
):
    slots = basis_ref.shape[0]
    width = pair_ref.shape[0]
    rank = rank_ref[0]
    row_ids = lax.broadcasted_iota(jnp.int32, (slots, slots), 0)
    lane_ids = lax.broadcasted_iota(jnp.int32, (slots, slots), 1)
    basis = basis_ref[...]
    pair = pair_ref[...]
    leaf_state = ridged(basis, rank, rank.astype(jnp.float32), row_ids, lane_ids)
    pair_state = ridged(pair, width, float(width), row_ids, lane_ids)

    def step(k, states):
        return tuple(eliminate(state, k, row_ids, lane_ids) for state in states)

    leaf_state, pair_state = lax.fori_loop(0, slots, step, (leaf_state, pair_state))
    leaf_weights = jnp.dot(
        leaf_state, basis, precision=HIGHEST, preferred_element_type=jnp.float32
    )
    pair_weights = jnp.dot(pair_state, pair, precision=HIGHEST, preferred_element_type=jnp.float32)
    pair_out_ref[...] = last_dims(upward_ref[...], pair_weights)
    leaf_out_ref[...] = last_dims(off_ref[...], leaf_weights)


def interpolate_both(rank, off, basis, upward, pair):
    vmem = pl.BlockSpec(memory_space=pltpu.VMEM)
    return pl.pallas_call(
        interpolate_kernel,
        in_specs=[pl.BlockSpec(memory_space=pltpu.SMEM)] + [vmem] * 4,
        out_specs=[vmem] * 2,
        out_shape=[
            jax.ShapeDtypeStruct((off.shape[0], basis.shape[0]), jnp.float32),
            jax.ShapeDtypeStruct((upward.shape[0], pair.shape[0]), jnp.float32),
        ],
        compiler_params=pltpu.CompilerParams(vmem_limit_bytes=32 * 2**20),
        name="interpolate_both",
    )(rank, off, basis, upward, pair)


def body(
    front_matrix, random_probe, child_samples, child_dest, skeleton, leaf_ranks, pair_skeleton
):
    matrix = front_matrix[0]
    own_probe = random_probe[0]
    height = matrix.shape[0]
    samples = own_probe.shape[1]
    half = samples // 2
    leaf_index = lax.axis_index("blk")
    me = leaf_index.astype(jnp.int32)[None]
    pair_index = leaf_index // 2
    lower_half = leaf_index % 2 == 0

    gathered = lax.all_gather(own_probe[:, :half], "blk", axis=0, tiled=True)
    partial = transposed_product(matrix, own_probe[:, half:].T, me)
    sibling_probe = from_partner(own_probe, "blk", 0)

    blocks = lax.axis_size("blk")
    incoming = child_samples[0]
    destinations = child_dest[0]
    count_rows = incoming.shape[0]
    capacity = max(2, (2 * count_rows + blocks - 1) // blocks)
    owner_block = destinations // height
    within = (destinations % height).astype(jnp.float32)
    order = jnp.arange(count_rows, dtype=jnp.int32)
    earlier = (owner_block[:, None] == owner_block[None, :]) & (order[None, :] < order[:, None])
    ranking = jnp.sum(earlier.astype(jnp.int32), axis=1)
    places = owner_block * capacity + ranking
    slots_total = blocks * capacity
    sending = jnp.zeros((slots_total, samples), jnp.float32).at[places].set(incoming)
    labels = jnp.full((slots_total,), float(height), jnp.float32).at[places].set(within)
    chosen = skeleton[0, 0]
    leaf_rank = leaf_ranks[0, 0]
    live_mask = (jnp.arange(chosen.shape[0]) < leaf_rank)[:, None]
    sibling_start = (leaf_index ^ 1) * height
    sibling_columns = lax.dynamic_slice_in_dim(matrix[chosen], sibling_start, height, 1)
    sibling_term = exact_dot(sibling_columns, sibling_probe)

    sending, sibling_term, partial = lax.optimization_barrier((sending, sibling_term, partial))
    upper_columns = lax.psum_scatter(partial, "blk", scatter_dimension=0, tiled=True)
    spread_rows, spread_labels = (
        lax.all_to_all(sending, "blk", split_axis=0, concat_axis=0, tiled=True),
        lax.all_to_all(labels, "blk", split_axis=0, concat_axis=0, tiled=True),
    )
    arrived, arrived_labels = from_behind((spread_rows, spread_labels), "front", 1)
    lower_columns = forward_product(matrix, gathered, me)
    arrived, arrived_labels, lower_columns = lax.optimization_barrier(
        (arrived, arrived_labels, lower_columns)
    )
    child_part = jax.ops.segment_sum(
        arrived, arrived_labels.astype(jnp.int32), num_segments=height + 1
    )[:height]

    off_sample = jnp.concatenate([lower_columns, upper_columns], axis=1) + child_part
    picked = off_sample[chosen]
    leaf_basis = jnp.where(live_mask, picked, 0.0)
    upward = jnp.where(live_mask, picked - sibling_term, 0.0)
    sibling = from_partner(upward, "blk", 0)
    stacked = jnp.where(
        lower_half, jnp.concatenate([upward, sibling]), jnp.concatenate([sibling, upward])
    )
    pick_rows = lax.dynamic_index_in_dim(pair_skeleton[0], pair_index, 0, keepdims=False)
    pair_basis = stacked[pick_rows]
    leaf_interp, pair_interp = interpolate_both(
        leaf_rank[None], off_sample, leaf_basis, upward, pair_basis
    )
    return (leaf_interp[None], pair_interp[None])


def solution(mesh):
    placed = (
        P("front", "blk", None),
        P("front", "blk", None),
        P("front", "blk", None),
        P("front", "blk"),
        P("front", "blk", None),
        P("front", "blk"),
        P("front", None, None),
    )
    return jax.shard_map(
        body,
        mesh=mesh,
        in_specs=placed,
        out_specs=(P("front", "blk", None), P("front", "blk", None)),
        check_vma=False,
    )
```
